512 devices in a mesh: rows: 16 (over z, core), cols: 32 (over x, y).
Axes of the slice: x: 4, y: 8, z: 8, core: 2. Of those that a mesh axis runs over, the one named last changes fastest.
Arguments:
- left_query: bfloat16 [32, 4096, 256], P('rows', 'cols'), parts along dimension 0, may hold values from -16 to 16
- left_value: bfloat16 [32, 4096, 256], P('rows', 'cols'), parts along dimension 0, may hold values from -6 to 6
- right_key: bfloat16 [32, 4096, 256], P('rows', 'cols'), parts along dimension 0, may hold values from -16 to 16
- right_value: bfloat16 [32, 4096, 256], P('rows', 'cols'), parts along dimension 0, may hold values from -6 to 6
- bound: int32 [32], P('rows'), parts along dimension 0, may hold values from 0 to 31
Outputs:
- left_out: bfloat16 [32, 4096, 256], P('rows', 'cols'), parts along dimension 0
- right_out: bfloat16 [32, 4096, 256], P('rows', 'cols'), parts along dimension 0
The draws below stay inside these ranges and needn't reach their ends.
There are 16 independent parts, one for each index of `rows`. The reference program is written for one: setup_inputs(seed, part) draws one part's arguments, and reference() takes and returns one part's arrays. A program takes and returns all parts, laid end to end along the dimension named above; each array names one. Nothing has to cross between parts.
All inputs are finite; a program needn't handle non-finite values.
Results may differ from the reference program's by a relative error of at most 0.0045.
Values may be sent and summed in bfloat16 or wider, within the bound.
A program may use at most 64 MiB of HBM per device.

```python
import math
import jax
import jax.numpy as jnp
from jax import lax

D = 256
ROWS = 2
COL_DEV = 128
W = 4096
N_COLS = 32


def draw_pair(key):
    base = jax.random.fold_in(key, 11)
    key_q, key_k = jax.random.split(base, 2)
    queries = jnp.clip(jax.random.normal(key_q, (ROWS, W, D)) * 1.7, -10.0, 10.0)
    keys = jnp.clip(jax.random.normal(key_k, (ROWS, W, D)) * 1.7, -10.0, 10.0)
    return (jnp.clip(queries, -16.0, 16.0), jnp.clip(keys, -16.0, 16.0))


def draw_left_query(key, part):
    return draw_pair(key)[0].astype(jnp.bfloat16)


def draw_right_key(key, part):
    return draw_pair(key)[1].astype(jnp.bfloat16)


def block_scale(own_key, extent, cuts, smallest, largest):
    factor_of = 1.0
    for position, blocks in cuts:
        draws = jax.random.uniform(jax.random.fold_in(jax.random.fold_in(own_key, 6), position), (blocks,), jnp.float32, smallest / len(cuts), largest / len(cuts))
        factor_of = factor_of * jnp.repeat(jnp.exp(draws), extent[position] // blocks).reshape((-1,) + (1,) * (len(extent) - 1 - position))
    return factor_of


def bell_draw(stream_key, dims, spread, limit, cuts=(), held_as=jnp.bfloat16):
    values = jax.random.normal(stream_key, dims, jnp.float32) * spread
    if len(cuts) > 0:
        values = block_scale(stream_key, dims, cuts, -0.22, 0.18) * values
    return jnp.clip(values, min=-limit, max=limit).astype(held_as)


def setup_inputs(seed: int = 0, part: int = 0) -> dict:
    arg_keys = jax.random.split(jax.random.key(seed), 6)
    part_keys = jax.random.split(jax.random.fold_in(arg_keys[5], part), 6)
    left_query = draw_left_query(jax.random.fold_in(jax.random.fold_in(arg_keys[5], part), 71), part)
    left_value = bell_draw(part_keys[1], (ROWS, W, D), 1.0, 6.0, ((1, 32),))
    right_key = draw_right_key(jax.random.fold_in(jax.random.fold_in(arg_keys[5], part), 71), part)
    right_value = bell_draw(part_keys[3], (ROWS, W, D), 1.0, 6.0, ((1, 32),))
    bound = jax.random.randint(part_keys[4], (ROWS,), 0, N_COLS).astype(jnp.int32)
    return {"left_query": left_query, "left_value": left_value, "right_key": right_key, "right_value": right_value, "bound": bound}


def attend_view(own, others, other_values, bound, lower_side):
    block = math.gcd(512, W)
    count = W // block
    pieces = jnp.transpose(own.reshape(ROWS, count, block, D), (1, 0, 2, 3))
    other_pos = jnp.arange(W, dtype=jnp.int32)
    reach = bound[:, None, None]
    scale = 1.0 / math.sqrt(D)

    def one_block(index_and_piece):
        index, piece = index_and_piece
        scores = jnp.einsum('rqd,rkd->rqk', piece.astype(jnp.float32), others.astype(jnp.float32)) * scale
        own_pos = index * block + jnp.arange(block, dtype=jnp.int32)
        if lower_side:
            valid = (other_pos[None, None, :] <= own_pos[None, :, None]) & ((own_pos // COL_DEV)[None, :, None] - (other_pos // COL_DEV)[None, None, :] <= reach)
        else:
            valid = (other_pos[None, None, :] >= own_pos[None, :, None]) & ((other_pos // COL_DEV)[None, None, :] - (own_pos // COL_DEV)[None, :, None] <= reach)
        top = lax.optimization_barrier(jnp.max(jnp.where(valid, scores, -1e+30), axis=-1, keepdims=True))
        weights = jnp.where(valid, jnp.exp(scores - top), 0.0)
        total = lax.optimization_barrier(jnp.sum(weights, axis=-1))
        rounded = weights.astype(jnp.bfloat16).astype(jnp.float32)
        summed = jnp.einsum('rqk,rkd->rqd', rounded, other_values.astype(jnp.float32))
        return (summed / total[:, :, None]).astype(jnp.bfloat16)
    outs = lax.map(one_block, (jnp.arange(count, dtype=jnp.int32), pieces))
    return jnp.transpose(outs, (1, 0, 2, 3)).reshape(ROWS, W, D)

def reference(left_query, left_value, right_key, right_value, bound):
    left_out = attend_view(left_query, right_key, right_value, bound, True)
    right_out = attend_view(right_key, left_query, left_value, bound, False)
    return (left_out, right_out)
```

```python
import jax
import jax.numpy as jnp
from jax import lax
from jax.experimental import pallas as pl
from jax.experimental.pallas import tpu as pltpu
from jax.sharding import PartitionSpec as P

MESH = pl.DeviceIdType.MESH
F32 = jnp.float32
BF16 = jnp.bfloat16

NX, NY = 4, 8
T, D = 128, 256
STAT = 16
MSG = D + STAT
NEVER = -(2.0**100)
FAR = 1 << 28
SCALE = 1.4426950408889634 / 16.0

AP, B1P, B1M, B2, AX = 0, 1, 2, 3, 4
PAX, PAP, PBF, PBP, PBM = 14, 17, 18, 19, 20
KINDS = 21


def kernel(
    bound_ref, lq, lv, rk, rv, lo, ro,
    ak, av, bk, bv, raw, pa_w, pb_w, sa, sb, oa, ob, stat_a, stat_b,
    pa, ra, passed, rap, pb, rb, send, recv, local,
):
    row = lax.axis_index("rows")
    col = lax.axis_index("cols")
    x, y = col // NY, col % NY

    def at(nx, ny):
        return (row, nx * NY + ny)

    def step_y(d):
        return lax.rem(y + d + NY, NY)

    odd = lax.rem(y, 2)
    partner = [step_y(1 - 2 * odd), step_y(2 * odd - 1)]
    up, down = at(x, step_y(2)), at(x, step_y(-2))
    mate = [at(x, partner[0]), at(x, partner[1])]
    across = [at(lax.rem(x + d, NX), y) for d in (1, 2, 3)]

    keys_a, keys_b = (lq.at[0], rk.at[1]), (rk.at[0], lq.at[1])
    vals_a, vals_b = (lv.at[0], rv.at[1]), (rv.at[0], lv.at[1])
    out_a, out_b = (lo.at[0], ro.at[1]), (ro.at[0], lo.at[1])
    lines = [NX - x, x + 1]

    barrier = pltpu.get_barrier_semaphore()
    for device in [up, down] + mate + across:
        pl.semaphore_signal(barrier, inc=1, device_id=device, device_id_type=MESH)

    copies = []
    for t in range(2):
        for src, dst in (
            (keys_a[t], ak.at[t, 0, pl.ds(0, T)]),
            (keys_b[t], bk.at[t, pl.ds(0, T)]),
            (vals_a[t], raw.at[t, 0]),
            (vals_b[t], raw.at[t, 1]),
        ):
            copies.append(pltpu.make_async_copy(src, dst, local.at[len(copies)]))
            copies[-1].start()
    for copy in copies:
        copy.wait()
    for t in range(2):
        av[t, 0, 0] = raw[t, 0].astype(F32).T.astype(BF16)
        bv[t, 0] = raw[t, 1].astype(F32).T.astype(BF16)

    pl.semaphore_wait(barrier, 7)

    def message(t, number, src, dst, device):
        n = t * KINDS + number
        return pltpu.make_async_remote_copy(
            src_ref=src, dst_ref=dst, send_sem=send.at[n], recv_sem=recv.at[n],
            device_id=device, device_id_type=MESH,
        )

    def line(t, d):
        return at(x - d, y) if t == 0 else at(x + d, y)

    def line_in(t, d):
        return x - d >= 0 if t == 0 else x + d < NX

    def ap(t, kv):
        if kv == 0:
            return message(t, AP, ak.at[t, 0, pl.ds(0, T)], ak.at[t, 0, pl.ds(T, T)], mate[t])
        return message(t, 7 + AP, av.at[t, 0, 0], av.at[t, 0, 1], mate[t])

    def b_slot(t, kv, s):
        return bk.at[t, pl.ds(s * T, T)] if kv == 0 else bv.at[t, s]

    def b1p(t, kv):
        return message(t, 7 * kv + B1P, b_slot(t, kv, 0), b_slot(t, kv, 1), up)

    def b1m(t, kv):
        return message(t, 7 * kv + B1M, b_slot(t, kv, 0), b_slot(t, kv, 2), down)

    def b2(t, kv):
        return message(
            t, 7 * kv + B2, b_slot(t, kv, 1 + t), b_slot(t, kv, 3), up if t == 0 else down
        )

    def ax(t, kv, d):
        ref = ak if kv == 0 else av
        return message(t, 7 * kv + AX + d - 1, ref.at[t, 0], ref.at[t, d], line(t, d))

    def pax(t, d):
        return message(t, PAX + d - 1, pa.at[t, d], ra.at[t, d], line(t, -d))

    def pap(t):
        return message(t, PAP, passed.at[t], rap.at[t], mate[t])

    def arrival(t, number, src, dst):
        return message(t, number, src, dst, up)

    def pbf(t):
        return message(t, PBF, pb.at[t, 3], rb.at[t, 0], up if t == 0 else down)

    def pbp(t):
        return message(t, PBP, pb.at[t, 2], rb.at[t, 1], up)

    def pbm(t):
        return message(t, PBM, pb.at[t, 1], rb.at[t, 2], down)

    def each_line(t, act, kv):
        for d in (1, 2, 3):
            pl.when(line_in(t, d))(lambda d=d: act(ax(t, kv, d)))

    def start(m):
        m.start()

    def relay_b(t, kv):
        (b1p if t == 0 else b1m)(t, kv).wait_recv()
        b2(t, kv).start()

    def rest_b(t, kv):
        (b1m if t == 0 else b1p)(t, kv).wait_recv()
        b2(t, kv).wait_recv()

    for t in range(2):
        ap(t, 0).start()
    for t in range(2):
        b1p(t, 0).start()
        b1m(t, 0).start()
    for t in range(2):
        ap(t, 1).start()
    b1p(0, 1).start()
    b1m(0, 1).start()
    for t in range(2):
        ap(t, 0).wait_recv()
        each_line(t, start, 0)
    for t in range(2):
        relay_b(t, 0)
    b1p(1, 1).start()
    b1m(1, 1).start()
    for t in range(2):
        ap(t, 1).wait_recv()
        each_line(t, start, 1)

    y_b = [y, step_y(-2), step_y(2), step_y(4)]
    diff = lax.broadcasted_iota(jnp.int32, (T, T), 1) - lax.broadcasted_iota(jnp.int32, (T, T), 0)

    def threshold(t, d, s, h):
        y_a = partner[t] if h else y
        ahead = 8 * d + (y_a - y_b[s] if t == 0 else y_b[s] - y_a)
        return jnp.where(ahead <= bound_ref[t], -T * ahead, FAR)

    def scores(t):
        @pl.loop(0, lines[t])
        def _(d):
            @pl.when(d > 0)
            def _():
                arrival(t, AX + d - 1, ak.at[t, 0], ak.at[t, d]).wait_recv()

            a = ak[t, d]
            top = jnp.full((1, 2 * T), NEVER, F32)
            for s in range(4):
                dots = lax.dot_general(
                    bk[t, pl.ds(s * T, T)], a, (((1,), (1,)), ((), ())), preferred_element_type=F32
                ) * SCALE
                for h in range(2):
                    gap = diff if t == 0 else -diff
                    piece = jnp.where(
                        gap >= threshold(t, d, s, h), dots[:, h * T : (h + 1) * T], NEVER
                    )
                    sa[pl.ds(s * T, T), pl.ds(h * T, T)] = piece
            for s in range(4):
                top = jnp.maximum(top, jnp.max(sa[pl.ds(s * T, T)], axis=0, keepdims=True))
            top = top.astype(BF16).astype(F32)
            total = jnp.zeros((1, 2 * T), F32)
            for s in range(4):
                w = jnp.exp2(sa[pl.ds(s * T, T)] - top)
                total = total + jnp.sum(w, axis=0, keepdims=True)
                pa_w[t, d, pl.ds(s * T, T)] = w.astype(BF16)
            stat_a[t, d, 0:1] = top
            stat_a[t, d, 1:2] = total
            for s in range(4):
                dots = lax.dot_general(
                    a, bk[t, pl.ds(s * T, T)], (((1,), (1,)), ((), ())), preferred_element_type=F32
                ) * SCALE
                for h in range(2):
                    gap = -diff if t == 0 else diff
                    sb[d, pl.ds(h * T, T), pl.ds(s * T, T)] = jnp.where(
                        gap >= threshold(t, d, s, h), dots[h * T : (h + 1) * T], NEVER
                    )

        top = lax.fori_loop(
            0, lines[t],
            lambda d, m: jnp.maximum(m, jnp.max(sb[d], axis=0, keepdims=True)),
            jnp.full((1, 4 * T), NEVER, F32),
        )
        top = top.astype(BF16).astype(F32)

        def weigh(d, total):
            w = jnp.exp2(sb[d] - top)
            pb_w[t, d] = w.astype(BF16)
            return total + jnp.sum(w, axis=0, keepdims=True)

        total = lax.fori_loop(0, lines[t], weigh, jnp.zeros((1, 4 * T), F32))
        stat_b[t, 0:1] = top
        stat_b[t, 1:2] = total

    for t in range(2):
        rest_b(t, 0)
        scores(t)
        relay_b(t, 1)

    def put(ref, top, total, rows):
        place = lax.broadcasted_iota(jnp.int32, (STAT, rows.shape[1]), 0)
        ref[pl.ds(0, D)] = rows.astype(BF16)
        high = total.astype(BF16).astype(F32)
        stats = jnp.where(place == 0, top, jnp.where(place == 1, high, jnp.where(place == 2, total - high, 0.0)))
        ref[pl.ds(D, STAT)] = stats.astype(BF16)

    def get(ref):
        stats = ref[pl.ds(D, STAT)].astype(F32)
        return stats[0:1], stats[1:2] + stats[2:3], ref[pl.ds(0, D)].astype(F32)

    def b_part(t, s):
        c = pl.ds(s * T, T)
        return stat_b[t, 0:1, c], stat_b[t, 1:2, c], ob[t, :, c]

    def merge(one, two):
        top = jnp.maximum(one[0], two[0])
        a, b = jnp.exp2(one[0] - top), jnp.exp2(two[0] - top)
        return top, one[1] * a + two[1] * b, one[2] * a + two[2] * b

    for t in range(2):
        ob[t] = jnp.zeros_like(ob[t])

        @pl.loop(0, lines[t])
        def _(d, t=t):
            @pl.when(d > 0)
            def _():
                arrival(t, 7 + AX + d - 1, av.at[t, 0], av.at[t, d]).wait_recv()

            values = jnp.concatenate([av[t, d, 0], av[t, d, 1]], axis=1)
            ob[t] += jnp.dot(values, pb_w[t, d], preferred_element_type=F32)

        put(pb.at[t, 3], *b_part(t, 3))
        pbf(t).start()
        put(pb.at[t, 1 + t], *b_part(t, 1 + t))
        (pbm if t == 0 else pbp)(t).start()

    for t in range(2):
        rest_b(t, 1)

        @pl.loop(0, lines[t])
        def _(d, t=t):
            values = jnp.concatenate([bv[t, s] for s in range(4)], axis=1)
            rows = jnp.dot(values, pa_w[t, d], preferred_element_type=F32)

            @pl.when(d == 0)
            def _():
                oa[t] = rows

            @pl.when(d > 0)
            def _():
                put(pa.at[t, d], stat_a[t, d, 0:1], stat_a[t, d, 1:2], rows)
                pax(t, d).start()

    for t in range(2):
        pbf(t).wait_recv()
        put(pb.at[t, 2 - t], *merge(b_part(t, 2 - t), get(rb.at[t, 0])))
        (pbp if t == 0 else pbm)(t).start()

    for t in range(2):

        @pl.loop(1, NX + 1 - lines[t])
        def _(d, t=t):
            arrival(t, PAX + d - 1, pa.at[t, d], ra.at[t, d]).wait_recv()
            top, total, rows = merge((stat_a[t, 0, 0:1], stat_a[t, 0, 1:2], oa[t]), get(ra.at[t, d]))
            stat_a[t, 0, 0:1] = top
            stat_a[t, 0, 1:2] = total
            oa[t] = rows

        put(passed.at[t], stat_a[t, 0, 0:1, T:], stat_a[t, 0, 1:2, T:], oa[t, :, T:])
        pap(t).start()

    def finish(ref, part):
        ref[...] = (part[2] * (1.0 / part[1])).T.astype(BF16)

    for t in range(2):
        pbp(t).wait_recv()
        pbm(t).wait_recv()
        finish(out_b[t], merge(merge(b_part(t, 0), get(rb.at[t, 1])), get(rb.at[t, 2])))
    for t in range(2):
        pap(t).wait_recv()
        own = stat_a[t, 0, 0:1, :T], stat_a[t, 0, 1:2, :T], oa[t, :, :T]
        finish(out_a[t], merge(own, get(rap.at[t])))

    for t in range(2):
        for kv in range(2):
            for m in (ap, b1p, b1m, b2):
                m(t, kv).wait_send()
            each_line(t, lambda m: m.wait_send(), kv)
        for m in (pbf, pbp, pbm, pap):
            m(t).wait_send()

        @pl.loop(1, lines[t])
        def _(d, t=t):
            pax(t, d).wait_send()


def body(left_query, left_value, right_key, right_value, bound):
    hbm = pl.BlockSpec(memory_space=pl.ANY)
    vmem = pl.BlockSpec(memory_space=pltpu.VMEM)
    out = jax.ShapeDtypeStruct((2, T, D), BF16)
    return pl.pallas_call(
        kernel,
        out_shape=(out, out),
        in_specs=[pl.BlockSpec(memory_space=pltpu.SMEM), hbm, hbm, hbm, hbm],
        out_specs=(vmem, vmem),
        scratch_shapes=[
            pltpu.VMEM((2, NX, 2 * T, D), BF16),
            pltpu.VMEM((2, NX, 2, D, T), BF16),
            pltpu.VMEM((2, 4 * T, D), BF16),
            pltpu.VMEM((2, 4, D, T), BF16),
            pltpu.VMEM((2, 2, T, D), BF16),
            pltpu.VMEM((2, NX, 4 * T, 2 * T), BF16),
            pltpu.VMEM((2, NX, 2 * T, 4 * T), BF16),
            pltpu.VMEM((4 * T, 2 * T), F32),
            pltpu.VMEM((NX, 2 * T, 4 * T), F32),
            pltpu.VMEM((2, D, 2 * T), F32),
            pltpu.VMEM((2, D, 4 * T), F32),
            pltpu.VMEM((2, NX, 8, 2 * T), F32),
            pltpu.VMEM((2, 8, 4 * T), F32),
            pltpu.VMEM((2, NX, MSG, 2 * T), BF16),
            pltpu.VMEM((2, NX, MSG, 2 * T), BF16),
            pltpu.VMEM((2, MSG, T), BF16),
            pltpu.VMEM((2, MSG, T), BF16),
            pltpu.VMEM((2, 4, MSG, T), BF16),
            pltpu.VMEM((2, 3, MSG, T), BF16),
            pltpu.SemaphoreType.DMA((2 * KINDS,)),
            pltpu.SemaphoreType.DMA((2 * KINDS,)),
            pltpu.SemaphoreType.DMA((8,)),
        ],
        compiler_params=pltpu.CompilerParams(
            collective_id=0, has_side_effects=True, vmem_limit_bytes=48 * 1024 * 1024
        ),
    )(bound, left_query, left_value, right_key, right_value)


def solution(mesh):
    placed = P("rows", "cols", None)
    return jax.shard_map(
        body,
        mesh=mesh,
        in_specs=(placed, placed, placed, placed, P("rows")),
        out_specs=(placed, placed),
        check_vma=False,
    )
```

```python
import jax
import jax.numpy as jnp
from jax import lax
from jax.experimental import pallas as pl
from jax.experimental.pallas import tpu as pltpu
from jax.sharding import PartitionSpec as P

MESH = pl.DeviceIdType.MESH
F32 = jnp.float32
BF16 = jnp.bfloat16

NX, NY = 4, 8
T, D = 128, 256
STAT = 16
MSG = D + STAT
NEVER = -(2.0**100)
FAR = 1 << 28
SCALE = 1.4426950408889634 / 16.0

AP, B1P, B1M, B2P, B2M, AX = 0, 1, 2, 3, 4, 5
VALUES = 8
PAX, PAP, PBF, PBP, PBM = 16, 22, 23, 24, 25
KINDS = 26


def kernel(
    bound, lq, lv, rk, rv, out,
    ak, av, bk, bv, raw, pa_w, pb_w, sa, sb, oa, ob, stat_a, stat_b,
    pa, ra, passed, rap, pb, rb, bound_ref, send, recv, local,
):
    row = lax.axis_index("rows")
    col = lax.axis_index("cols")
    x, y = col // NY, col % NY

    def at(nx, ny):
        return (row, nx * NY + ny)

    def step_y(d):
        return lax.rem(y + d + NY, NY)

    odd = lax.rem(y, 2)
    partner = [step_y(1 - 2 * odd), step_y(2 * odd - 1)]
    up, down = at(x, step_y(2)), at(x, step_y(-2))
    mate = [at(x, partner[0]), at(x, partner[1])]
    across = [at(lax.rem(x + d, NX), y) for d in (1, 2, 3)]

    keys_a, keys_b = (lq.at[0], rk.at[1]), (rk.at[0], lq.at[1])
    vals_a, vals_b = (lv.at[0], rv.at[1]), (rv.at[0], lv.at[1])
    out_a, out_b = (out.at[0], out.at[3]), (out.at[2], out.at[1])
    lines = [NX - x, x + 1]

    barrier = pltpu.get_barrier_semaphore()
    for device in [up, down] + mate + across:
        pl.semaphore_signal(barrier, inc=1, device_id=device, device_id_type=MESH)

    copies = []
    for t in range(2):
        for src, dst in (
            (keys_a[t], ak.at[t, 0, pl.ds(0, T)]),
            (keys_b[t], bk.at[t, pl.ds(0, T)]),
            (vals_a[t], raw.at[t, 0]),
            (vals_b[t], raw.at[t, 1]),
        ):
            copies.append(pltpu.make_async_copy(src, dst, local.at[len(copies)]))
            copies[-1].start()
    copies.append(pltpu.make_async_copy(bound, bound_ref, local.at[8]))
    copies[-1].start()
    pl.semaphore_wait(barrier, 7)

    def message(t, number, src, dst, device):
        n = t * KINDS + number
        return pltpu.make_async_remote_copy(
            src_ref=src, dst_ref=dst, send_sem=send.at[n], recv_sem=recv.at[n],
            device_id=device, device_id_type=MESH,
        )

    def line(t, d):
        return at(x - d, y) if t == 0 else at(x + d, y)

    def line_in(t, d):
        return x - d >= 0 if t == 0 else x + d < NX

    def ap(t, kv):
        if kv == 0:
            return message(t, AP, keys_a[t], ak.at[t, 0, pl.ds(T, T)], mate[t])
        return message(t, VALUES + AP, av.at[t, 0, 0], av.at[t, 0, 1], mate[t])

    def b_slot(t, kv, s):
        return bk.at[t, pl.ds(s * T, T)] if kv == 0 else bv.at[t, s]

    def b_own(t, kv):
        return keys_b[t] if kv == 0 else bv.at[t, 0]

    def b1p(t, kv):
        return message(t, VALUES * kv + B1P, b_own(t, kv), b_slot(t, kv, 1), up)

    def b1m(t, kv):
        return message(t, VALUES * kv + B1M, b_own(t, kv), b_slot(t, kv, 2), down)

    def b_half(t, kv, s, half):
        if kv == 0:
            return bk.at[t, pl.ds(s * T + half * (T // 2), T // 2)]
        return bv.at[t, s, pl.ds(half * (D // 2), D // 2)]

    def b2p(t, kv):
        return message(t, VALUES * kv + B2P, b_half(t, kv, 1, 0), b_half(t, kv, 3, 0), up)

    def b2m(t, kv):
        return message(t, VALUES * kv + B2M, b_half(t, kv, 2, 1), b_half(t, kv, 3, 1), down)

    def ax(t, kv, d):
        ref = ak if kv == 0 else av
        return message(t, VALUES * kv + AX + d - 1, ref.at[t, 0], ref.at[t, d], line(t, d))

    def pax(t, d, h):
        return message(t, PAX + 3 * h + d - 1, pa.at[t, d, h], ra.at[t, d, h], line(t, -d))

    def pap(t):
        return message(t, PAP, passed.at[t], rap.at[t], mate[t])

    def arrival(t, number, src, dst):
        return message(t, number, src, dst, up)

    def pbf(t):
        return message(t, PBF, pb.at[t, 3], rb.at[t, 0], up if t == 0 else down)

    def pbp(t):
        return message(t, PBP, pb.at[t, 2], rb.at[t, 1], up)

    def pbm(t):
        return message(t, PBM, pb.at[t, 1], rb.at[t, 2], down)

    def each_line(t, act, kv):
        for d in (1, 2, 3):
            pl.when(line_in(t, d))(lambda d=d: act(ax(t, kv, d)))

    def start(m):
        m.start()

    def load():
        for copy in copies:
            copy.wait()
        for t in range(2):
            av[t, 0, 0] = raw[t, 0].astype(F32).T.astype(BF16)
            bv[t, 0] = raw[t, 1].astype(F32).T.astype(BF16)

    def send_a(t, kv):
        ap(t, kv).start()

    def send_b(t, kv):
        b1p(t, kv).start()
        b1m(t, kv).start()

    def relay_a(t, kv):
        ap(t, kv).wait_recv()
        each_line(t, start, kv)

    def relay_b(t, kv):
        b1p(t, kv).wait_recv()
        b2p(t, kv).start()
        b1m(t, kv).wait_recv()
        b2m(t, kv).start()

    def rest_b(t, kv):
        b2p(t, kv).wait_recv()
        b2m(t, kv).wait_recv()

    y_b = [y, step_y(-2), step_y(2), step_y(4)]
    diff = lax.broadcasted_iota(jnp.int32, (T, T), 1) - lax.broadcasted_iota(jnp.int32, (T, T), 0)

    def threshold(t, d, s, h):
        y_a = partner[t] if h else y
        ahead = 8 * d + (y_a - y_b[s] if t == 0 else y_b[s] - y_a)
        return jnp.where(ahead <= bound_ref[t], -T * ahead, FAR)

    def scores(t):
        @pl.loop(0, lines[t])
        def _(d):
            @pl.when(d > 0)
            def _():
                arrival(t, AX + d - 1, ak.at[t, 0], ak.at[t, d]).wait_recv()

            a = ak[t, d]
            top = jnp.full((1, 2 * T), NEVER, F32)
            for s in range(4):
                dots = lax.dot_general(
                    bk[t, pl.ds(s * T, T)], a, (((1,), (1,)), ((), ())), preferred_element_type=F32
                ) * SCALE
                for h in range(2):
                    gap = diff if t == 0 else -diff
                    piece = jnp.where(
                        gap >= threshold(t, d, s, h), dots[:, h * T : (h + 1) * T], NEVER
                    )
                    sa[pl.ds(s * T, T), pl.ds(h * T, T)] = piece
            for s in range(4):
                top = jnp.maximum(top, jnp.max(sa[pl.ds(s * T, T)], axis=0, keepdims=True))
            top = top.astype(BF16).astype(F32)
            total = jnp.zeros((1, 2 * T), F32)
            for s in range(4):
                w = jnp.exp2(sa[pl.ds(s * T, T)] - top)
                total = total + jnp.sum(w, axis=0, keepdims=True)
                pa_w[t, d, pl.ds(s * T, T)] = w.astype(BF16)
            stat_a[t, d, 0:1] = top
            stat_a[t, d, 1:2] = total
            for s in range(4):
                dots = lax.dot_general(
                    a, bk[t, pl.ds(s * T, T)], (((1,), (1,)), ((), ())), preferred_element_type=F32
                ) * SCALE
                for h in range(2):
                    gap = -diff if t == 0 else diff
                    sb[d, pl.ds(h * T, T), pl.ds(s * T, T)] = jnp.where(
                        gap >= threshold(t, d, s, h), dots[h * T : (h + 1) * T], NEVER
                    )

        top = lax.fori_loop(
            0, lines[t],
            lambda d, m: jnp.maximum(m, jnp.max(sb[d], axis=0, keepdims=True)),
            jnp.full((1, 4 * T), NEVER, F32),
        )
        top = top.astype(BF16).astype(F32)

        def weigh(d, total):
            w = jnp.exp2(sb[d] - top)
            pb_w[t, d] = w.astype(BF16)
            return total + jnp.sum(w, axis=0, keepdims=True)

        total = lax.fori_loop(0, lines[t], weigh, jnp.zeros((1, 4 * T), F32))
        stat_b[t, 0:1] = top
        stat_b[t, 1:2] = total

    def put(ref, top, total, rows):
        place = lax.broadcasted_iota(jnp.int32, (STAT, rows.shape[1]), 0)
        ref[pl.ds(0, D)] = rows.astype(BF16)
        high = total.astype(BF16).astype(F32)
        stats = jnp.where(place == 0, top, jnp.where(place == 1, high, jnp.where(place == 2, total - high, 0.0)))
        ref[pl.ds(D, STAT)] = stats.astype(BF16)

    def get(ref):
        stats = ref[pl.ds(D, STAT)].astype(F32)
        return stats[0:1], stats[1:2] + stats[2:3], ref[pl.ds(0, D)].astype(F32)

    def b_part(t, s):
        c = pl.ds(s * T, T)
        return stat_b[t, 0:1, c], stat_b[t, 1:2, c], ob[t, :, c]

    def merge(one, two):
        top = jnp.maximum(one[0], two[0])
        a, b = jnp.exp2(one[0] - top), jnp.exp2(two[0] - top)
        return top, one[1] * a + two[1] * b, one[2] * a + two[2] * b

    def sums_b(t):
        ob[t] = jnp.zeros_like(ob[t])

        @pl.loop(0, lines[t])
        def _(d, t=t):
            @pl.when(d > 0)
            def _():
                arrival(t, VALUES + AX + d - 1, av.at[t, 0], av.at[t, d]).wait_recv()

            values = jnp.concatenate([av[t, d, 0], av[t, d, 1]], axis=1)
            ob[t] += jnp.dot(values, pb_w[t, d], preferred_element_type=F32)

        put(pb.at[t, 3], *b_part(t, 3))
        pbf(t).start()
        put(pb.at[t, 1 + t], *b_part(t, 1 + t))
        (pbm if t == 0 else pbp)(t).start()

    def sums_a(t):
        @pl.loop(0, lines[t])
        def _(d, t=t):
            values = jnp.concatenate([bv[t, s] for s in range(4)], axis=1)
            rows = jnp.dot(values, pa_w[t, d], preferred_element_type=F32)

            @pl.when(d == 0)
            def _():
                oa[t] = rows

            @pl.when(d > 0)
            def _():
                for h in range(2):
                    c = slice(h * T, (h + 1) * T)
                    put(pa.at[t, d, h], stat_a[t, d, 0:1, c], stat_a[t, d, 1:2, c], rows[:, c])
                pax(t, d, 1).start()

    def own_a(t):
        @pl.loop(1, lines[t])
        def _(d):
            pax(t, d, 0).start()

    def pass_b(t):
        pbf(t).wait_recv()
        put(pb.at[t, 2 - t], *merge(b_part(t, 2 - t), get(rb.at[t, 0])))
        (pbp if t == 0 else pbm)(t).start()

    def add_a(t, h):
        c = slice(h * T, (h + 1) * T)

        @pl.loop(1, NX + 1 - lines[t])
        def _(d):
            arrival(t, PAX + 3 * h + d - 1, pa.at[t, d, h], ra.at[t, d, h]).wait_recv()
            own = stat_a[t, 0, 0:1, c], stat_a[t, 0, 1:2, c], oa[t, :, c]
            top, total, rows = merge(own, get(ra.at[t, d, h]))
            stat_a[t, 0, 0:1, c] = top
            stat_a[t, 0, 1:2, c] = total
            oa[t, :, c] = rows

    def pass_a(t):
        add_a(t, 1)
        put(passed.at[t], stat_a[t, 0, 0:1, T:], stat_a[t, 0, 1:2, T:], oa[t, :, T:])
        pap(t).start()

    def finish(ref, part):
        ref[...] = (part[2] * (1.0 / part[1])).T.astype(BF16)

    def last_b(t):
        pbp(t).wait_recv()
        pbm(t).wait_recv()
        finish(out_b[t], merge(merge(b_part(t, 0), get(rb.at[t, 1])), get(rb.at[t, 2])))
    def last_a(t):
        add_a(t, 0)
        pap(t).wait_recv()
        own = stat_a[t, 0, 0:1, :T], stat_a[t, 0, 1:2, :T], oa[t, :, :T]
        finish(out_a[t], merge(own, get(rap.at[t])))

    send_b(0, 0)
    send_b(1, 0)
    send_a(0, 0)
    send_a(1, 0)
    load()
    send_a(0, 1)
    send_a(1, 1)
    send_b(0, 1)
    send_b(1, 1)
    relay_a(0, 0)
    relay_a(1, 0)
    relay_b(0, 0)
    relay_b(1, 0)
    relay_a(0, 1)
    relay_a(1, 1)
    relay_b(0, 1)
    relay_b(1, 1)
    rest_b(0, 0)
    rest_b(1, 0)
    scores(0)
    scores(1)
    sums_b(0)
    sums_b(1)
    rest_b(0, 1)
    rest_b(1, 1)
    sums_a(0)
    sums_a(1)
    own_a(0)
    own_a(1)
    pass_b(0)
    pass_b(1)
    pass_a(0)
    pass_a(1)
    last_b(0)
    last_b(1)
    last_a(0)
    last_a(1)

    for t in range(2):
        for kv in range(2):
            for m in (ap, b1p, b1m, b2p, b2m):
                m(t, kv).wait_send()
            each_line(t, lambda m: m.wait_send(), kv)
        for m in (pbf, pbp, pbm, pap):
            m(t).wait_send()

        @pl.loop(1, lines[t])
        def _(d, t=t):
            pax(t, d, 0).wait_send()
            pax(t, d, 1).wait_send()


def body(left_query, left_value, right_key, right_value, bound):
    hbm = pl.BlockSpec(memory_space=pl.ANY)
    vmem = pl.BlockSpec(memory_space=pltpu.VMEM)
    both = pl.pallas_call(
        kernel,
        out_shape=jax.ShapeDtypeStruct((4, T, D), BF16),
        in_specs=[hbm] * 5,
        out_specs=vmem,
        scratch_shapes=[
            pltpu.VMEM((2, NX, 2 * T, D), BF16),
            pltpu.VMEM((2, NX, 2, D, T), BF16),
            pltpu.VMEM((2, 4 * T, D), BF16),
            pltpu.VMEM((2, 4, D, T), BF16),
            pltpu.VMEM((2, 2, T, D), BF16),
            pltpu.VMEM((2, NX, 4 * T, 2 * T), BF16),
            pltpu.VMEM((2, NX, 2 * T, 4 * T), BF16),
            pltpu.VMEM((4 * T, 2 * T), F32),
            pltpu.VMEM((NX, 2 * T, 4 * T), F32),
            pltpu.VMEM((2, D, 2 * T), F32),
            pltpu.VMEM((2, D, 4 * T), F32),
            pltpu.VMEM((2, NX, 8, 2 * T), F32),
            pltpu.VMEM((2, 8, 4 * T), F32),
            pltpu.VMEM((2, NX, 2, MSG, T), BF16),
            pltpu.VMEM((2, NX, 2, MSG, T), BF16),
            pltpu.VMEM((2, MSG, T), BF16),
            pltpu.VMEM((2, MSG, T), BF16),
            pltpu.VMEM((2, 4, MSG, T), BF16),
            pltpu.VMEM((2, 3, MSG, T), BF16),
            pltpu.SMEM((2,), jnp.int32),
            pltpu.SemaphoreType.DMA((2 * KINDS,)),
            pltpu.SemaphoreType.DMA((2 * KINDS,)),
            pltpu.SemaphoreType.DMA((9,)),
        ],
        compiler_params=pltpu.CompilerParams(
            collective_id=0, has_side_effects=True, vmem_limit_bytes=56 * 1024 * 1024
        ),
    )(bound, left_query, left_value, right_key, right_value)
    return both[:2], both[2:]


def solution(mesh):
    placed = P("rows", "cols", None)
    return jax.shard_map(
        body,
        mesh=mesh,
        in_specs=(placed, placed, placed, placed, P("rows")),
        out_specs=(placed, placed),
        check_vma=False,
    )
```

```python
import jax
import jax.numpy as jnp
from jax import lax
from jax.experimental import pallas as pl
from jax.experimental.pallas import tpu as pltpu
from jax.sharding import PartitionSpec as P

MESH = pl.DeviceIdType.MESH
F32 = jnp.float32
BF16 = jnp.bfloat16

NX, NY = 4, 8
T, D = 128, 256
STAT = 16
MSG = D + STAT
NEVER = -(2.0**100)
FAR = 1 << 28
SCALE = 1.4426950408889634 / 16.0

AP, B1P, B1M, B2P, B2M, AX = 0, 1, 2, 3, 4, 5
VALUES = 11
PAX, PAP, PBF, PBP, PBM = 22, 28, 29, 30, 31
KINDS = 32


def kernel(
    bound, lq, lv, rk, rv, out,
    ak, av, bk, bv, raw, pa_w, pb_w, sa, sb, oa, ob, stat_a, stat_b,
    pa, ra, passed, rap, pb, rb, bound_ref, send, recv, local,
):
    row = lax.axis_index("rows")
    col = lax.axis_index("cols")
    x, y = col // NY, col % NY

    def at(nx, ny):
        return (row, nx * NY + ny)

    def step_y(d):
        return lax.rem(y + d + NY, NY)

    odd = lax.rem(y, 2)
    partner = [step_y(1 - 2 * odd), step_y(2 * odd - 1)]
    up, down = at(x, step_y(2)), at(x, step_y(-2))
    mate = [at(x, partner[0]), at(x, partner[1])]
    across = [at(lax.rem(x + d, NX), y) for d in (1, 2, 3)]

    keys_a, keys_b = (lq.at[0], rk.at[1]), (rk.at[0], lq.at[1])
    vals_a, vals_b = (lv.at[0], rv.at[1]), (rv.at[0], lv.at[1])
    out_a, out_b = (out.at[0], out.at[3]), (out.at[2], out.at[1])
    lines = [NX - x, x + 1]

    barrier = pltpu.get_barrier_semaphore()
    for device in [up, down] + mate + across:
        pl.semaphore_signal(barrier, inc=1, device_id=device, device_id_type=MESH)

    copies = []
    for t in range(2):
        for src, dst in (
            (keys_a[t], ak.at[t, 0, pl.ds(0, T)]),
            (keys_b[t], bk.at[t, pl.ds(0, T)]),
            (vals_a[t], raw.at[t, 0]),
            (vals_b[t], raw.at[t, 1]),
        ):
            copies.append(pltpu.make_async_copy(src, dst, local.at[len(copies)]))
            copies[-1].start()
    copies.append(pltpu.make_async_copy(bound, bound_ref, local.at[8]))
    copies[-1].start()
    pl.semaphore_wait(barrier, 7)

    def message(t, number, src, dst, device):
        n = t * KINDS + number
        return pltpu.make_async_remote_copy(
            src_ref=src, dst_ref=dst, send_sem=send.at[n], recv_sem=recv.at[n],
            device_id=device, device_id_type=MESH,
        )

    def line(t, d):
        return at(x - d, y) if t == 0 else at(x + d, y)

    def line_in(t, d):
        return x - d >= 0 if t == 0 else x + d < NX

    def ap(t, kv):
        if kv == 0:
            return message(t, AP, keys_a[t], ak.at[t, 0, pl.ds(T, T)], mate[t])
        return message(t, VALUES + AP, av.at[t, 0, 0], av.at[t, 0, 1], mate[t])

    def b_slot(t, kv, s):
        return bk.at[t, pl.ds(s * T, T)] if kv == 0 else bv.at[t, s]

    def b_own(t, kv):
        return keys_b[t] if kv == 0 else bv.at[t, 0]

    def b1p(t, kv):
        return message(t, VALUES * kv + B1P, b_own(t, kv), b_slot(t, kv, 1), up)

    def b1m(t, kv):
        return message(t, VALUES * kv + B1M, b_own(t, kv), b_slot(t, kv, 2), down)

    def b_half(t, kv, s, half):
        if kv == 0:
            return bk.at[t, pl.ds(s * T + half * (T // 2), T // 2)]
        return bv.at[t, s, pl.ds(half * (D // 2), D // 2)]

    def b2p(t, kv):
        return message(t, VALUES * kv + B2P, b_half(t, kv, 1, 0), b_half(t, kv, 3, 0), up)

    def b2m(t, kv):
        return message(t, VALUES * kv + B2M, b_half(t, kv, 2, 1), b_half(t, kv, 3, 1), down)

    def a_half(t, kv, d, h):
        return ak.at[t, d, pl.ds(h * T, T)] if kv == 0 else av.at[t, d, h]

    def ax(t, kv, d, h):
        src = keys_a[t] if kv == 0 and h == 0 else a_half(t, kv, 0, h)
        return message(t, VALUES * kv + AX + 3 * h + d - 1, src, a_half(t, kv, d, h), line(t, d))

    def arrive_a(t, kv, d):
        for h in range(2):
            arrival(
                t, VALUES * kv + AX + 3 * h + d - 1, a_half(t, kv, 0, h), a_half(t, kv, d, h)
            ).wait_recv()

    def pax(t, d, h):
        return message(t, PAX + 3 * h + d - 1, pa.at[t, d, h], ra.at[t, d, h], line(t, -d))

    def pap(t):
        return message(t, PAP, passed.at[t], rap.at[t], mate[t])

    def arrival(t, number, src, dst):
        return message(t, number, src, dst, up)

    def pbf(t):
        return message(t, PBF, pb.at[t, 3], rb.at[t, 0], up if t == 0 else down)

    def pbp(t):
        return message(t, PBP, pb.at[t, 2], rb.at[t, 1], up)

    def pbm(t):
        return message(t, PBM, pb.at[t, 1], rb.at[t, 2], down)

    def each_line(t, act, kv, h):
        for d in (1, 2, 3):
            pl.when(line_in(t, d))(lambda d=d: act(ax(t, kv, d, h)))

    def start(m):
        m.start()

    def load():
        for copy in copies:
            copy.wait()
        for t in range(2):
            av[t, 0, 0] = raw[t, 0].astype(F32).T.astype(BF16)
            bv[t, 0] = raw[t, 1].astype(F32).T.astype(BF16)

    def send_a(t, kv):
        ap(t, kv).start()

    def send_b(t, kv):
        b1p(t, kv).start()
        b1m(t, kv).start()

    def relay_a(t, kv):
        ap(t, kv).wait_recv()
        each_line(t, start, kv, 1)

    def send_x(t, kv):
        each_line(t, start, kv, 0)

    def relay_b(t, kv):
        b1p(t, kv).wait_recv()
        b2p(t, kv).start()
        b1m(t, kv).wait_recv()
        b2m(t, kv).start()

    def rest_b(t, kv):
        b2p(t, kv).wait_recv()
        b2m(t, kv).wait_recv()

    y_b = [y, step_y(-2), step_y(2), step_y(4)]
    diff = lax.broadcasted_iota(jnp.int32, (T, T), 1) - lax.broadcasted_iota(jnp.int32, (T, T), 0)

    def threshold(t, d, s, h):
        y_a = partner[t] if h else y
        ahead = 8 * d + (y_a - y_b[s] if t == 0 else y_b[s] - y_a)
        return jnp.where(ahead <= bound_ref[t], -T * ahead, FAR)

    def scores(t):
        @pl.loop(0, lines[t])
        def _(d):
            @pl.when(d > 0)
            def _():
                arrive_a(t, 0, d)

            a = ak[t, d]
            top = jnp.full((1, 2 * T), NEVER, F32)
            for s in range(4):
                dots = lax.dot_general(
                    bk[t, pl.ds(s * T, T)], a, (((1,), (1,)), ((), ())), preferred_element_type=F32
                ) * SCALE
                for h in range(2):
                    gap = diff if t == 0 else -diff
                    piece = jnp.where(
                        gap >= threshold(t, d, s, h), dots[:, h * T : (h + 1) * T], NEVER
                    )
                    sa[pl.ds(s * T, T), pl.ds(h * T, T)] = piece
            for s in range(4):
                top = jnp.maximum(top, jnp.max(sa[pl.ds(s * T, T)], axis=0, keepdims=True))
            top = top.astype(BF16).astype(F32)
            total = jnp.zeros((1, 2 * T), F32)
            for s in range(4):
                w = jnp.exp2(sa[pl.ds(s * T, T)] - top)
                total = total + jnp.sum(w, axis=0, keepdims=True)
                pa_w[t, d, pl.ds(s * T, T)] = w.astype(BF16)
            stat_a[t, d, 0:1] = top
            stat_a[t, d, 1:2] = total
            for s in range(4):
                dots = lax.dot_general(
                    a, bk[t, pl.ds(s * T, T)], (((1,), (1,)), ((), ())), preferred_element_type=F32
                ) * SCALE
                for h in range(2):
                    gap = -diff if t == 0 else diff
                    sb[d, pl.ds(h * T, T), pl.ds(s * T, T)] = jnp.where(
                        gap >= threshold(t, d, s, h), dots[h * T : (h + 1) * T], NEVER
                    )

        top = lax.fori_loop(
            0, lines[t],
            lambda d, m: jnp.maximum(m, jnp.max(sb[d], axis=0, keepdims=True)),
            jnp.full((1, 4 * T), NEVER, F32),
        )
        top = top.astype(BF16).astype(F32)

        def weigh(d, total):
            w = jnp.exp2(sb[d] - top)
            pb_w[t, d] = w.astype(BF16)
            return total + jnp.sum(w, axis=0, keepdims=True)

        total = lax.fori_loop(0, lines[t], weigh, jnp.zeros((1, 4 * T), F32))
        stat_b[t, 0:1] = top
        stat_b[t, 1:2] = total

    def put(ref, top, total, rows):
        place = lax.broadcasted_iota(jnp.int32, (STAT, rows.shape[1]), 0)
        ref[pl.ds(0, D)] = rows.astype(BF16)
        high = total.astype(BF16).astype(F32)
        stats = jnp.where(place == 0, top, jnp.where(place == 1, high, jnp.where(place == 2, total - high, 0.0)))
        ref[pl.ds(D, STAT)] = stats.astype(BF16)

    def get(ref):
        stats = ref[pl.ds(D, STAT)].astype(F32)
        return stats[0:1], stats[1:2] + stats[2:3], ref[pl.ds(0, D)].astype(F32)

    def b_part(t, s):
        c = pl.ds(s * T, T)
        return stat_b[t, 0:1, c], stat_b[t, 1:2, c], ob[t, :, c]

    def merge(one, two):
        top = jnp.maximum(one[0], two[0])
        a, b = jnp.exp2(one[0] - top), jnp.exp2(two[0] - top)
        return top, one[1] * a + two[1] * b, one[2] * a + two[2] * b

    def sums_b(t):
        ob[t] = jnp.zeros_like(ob[t])

        @pl.loop(0, lines[t])
        def _(d, t=t):
            @pl.when(d > 0)
            def _():
                arrive_a(t, 1, d)

            values = jnp.concatenate([av[t, d, 0], av[t, d, 1]], axis=1)
            ob[t] += jnp.dot(values, pb_w[t, d], preferred_element_type=F32)

        put(pb.at[t, 3], *b_part(t, 3))
        pbf(t).start()

    def direct_b(t):
        put(pb.at[t, 1 + t], *b_part(t, 1 + t))
        (pbm if t == 0 else pbp)(t).start()

    def sums_a(t):
        @pl.loop(0, lines[t])
        def _(d, t=t):
            values = jnp.concatenate([bv[t, s] for s in range(4)], axis=1)
            rows = jnp.dot(values, pa_w[t, d], preferred_element_type=F32)

            @pl.when(d == 0)
            def _():
                oa[t] = rows

            @pl.when(d > 0)
            def _():
                for h in range(2):
                    c = slice(h * T, (h + 1) * T)
                    put(pa.at[t, d, h], stat_a[t, d, 0:1, c], stat_a[t, d, 1:2, c], rows[:, c])
                pax(t, d, 1).start()

    def own_a(t):
        @pl.loop(1, lines[t])
        def _(d):
            pax(t, d, 0).start()

    def pass_b(t):
        pbf(t).wait_recv()
        put(pb.at[t, 2 - t], *merge(b_part(t, 2 - t), get(rb.at[t, 0])))
        (pbp if t == 0 else pbm)(t).start()

    def add_a(t, h):
        c = slice(h * T, (h + 1) * T)

        @pl.loop(1, NX + 1 - lines[t])
        def _(d):
            arrival(t, PAX + 3 * h + d - 1, pa.at[t, d, h], ra.at[t, d, h]).wait_recv()
            own = stat_a[t, 0, 0:1, c], stat_a[t, 0, 1:2, c], oa[t, :, c]
            top, total, rows = merge(own, get(ra.at[t, d, h]))
            stat_a[t, 0, 0:1, c] = top
            stat_a[t, 0, 1:2, c] = total
            oa[t, :, c] = rows

    def pass_a(t):
        add_a(t, 1)
        put(passed.at[t], stat_a[t, 0, 0:1, T:], stat_a[t, 0, 1:2, T:], oa[t, :, T:])
        pap(t).start()

    def finish(ref, part):
        ref[...] = (part[2] * (1.0 / part[1])).T.astype(BF16)

    def last_b(t):
        pbp(t).wait_recv()
        pbm(t).wait_recv()
        finish(out_b[t], merge(merge(b_part(t, 0), get(rb.at[t, 1])), get(rb.at[t, 2])))
    def last_a(t):
        add_a(t, 0)
        pap(t).wait_recv()
        own = stat_a[t, 0, 0:1, :T], stat_a[t, 0, 1:2, :T], oa[t, :, :T]
        finish(out_a[t], merge(own, get(rap.at[t])))

    def left_b(t, kv):
        b1p(t, kv).wait_send()
        b1m(t, kv).wait_send()

    send_b(0, 0)
    send_b(1, 0)
    send_a(0, 0)
    send_a(1, 0)
    send_x(0, 0)
    send_x(1, 0)
    load()
    send_a(0, 1)
    send_a(1, 1)
    send_x(0, 1)
    send_x(1, 1)
    send_b(0, 1)
    send_b(1, 1)
    relay_a(0, 0)
    relay_a(1, 0)
    relay_a(0, 1)
    relay_a(1, 1)
    relay_b(0, 0)
    relay_b(1, 0)
    relay_b(0, 1)
    relay_b(1, 1)
    rest_b(0, 0)
    rest_b(1, 0)
    scores(0)
    scores(1)
    sums_b(0)
    sums_b(1)
    rest_b(0, 1)
    rest_b(1, 1)
    sums_a(0)
    sums_a(1)
    own_a(0)
    own_a(1)
    direct_b(0)
    direct_b(1)
    pass_b(0)
    pass_b(1)
    pass_a(0)
    pass_a(1)
    last_b(0)
    last_b(1)
    last_a(0)
    last_a(1)

    for t in range(2):
        for kv in range(2):
            for m in (ap, b1p, b1m, b2p, b2m):
                m(t, kv).wait_send()
            for h in range(2):
                each_line(t, lambda m: m.wait_send(), kv, h)
        for m in (pbf, pbp, pbm, pap):
            m(t).wait_send()

        @pl.loop(1, lines[t])
        def _(d, t=t):
            pax(t, d, 0).wait_send()
            pax(t, d, 1).wait_send()


def body(left_query, left_value, right_key, right_value, bound):
    hbm = pl.BlockSpec(memory_space=pl.ANY)
    vmem = pl.BlockSpec(memory_space=pltpu.VMEM)
    both = pl.pallas_call(
        kernel,
        out_shape=jax.ShapeDtypeStruct((4, T, D), BF16),
        in_specs=[hbm] * 5,
        out_specs=vmem,
        scratch_shapes=[
            pltpu.VMEM((2, NX, 2 * T, D), BF16),
            pltpu.VMEM((2, NX, 2, D, T), BF16),
            pltpu.VMEM((2, 4 * T, D), BF16),
            pltpu.VMEM((2, 4, D, T), BF16),
            pltpu.VMEM((2, 2, T, D), BF16),
            pltpu.VMEM((2, NX, 4 * T, 2 * T), BF16),
            pltpu.VMEM((2, NX, 2 * T, 4 * T), BF16),
            pltpu.VMEM((4 * T, 2 * T), F32),
            pltpu.VMEM((NX, 2 * T, 4 * T), F32),
            pltpu.VMEM((2, D, 2 * T), F32),
            pltpu.VMEM((2, D, 4 * T), F32),
            pltpu.VMEM((2, NX, 8, 2 * T), F32),
            pltpu.VMEM((2, 8, 4 * T), F32),
            pltpu.VMEM((2, NX, 2, MSG, T), BF16),
            pltpu.VMEM((2, NX, 2, MSG, T), BF16),
            pltpu.VMEM((2, MSG, T), BF16),
            pltpu.VMEM((2, MSG, T), BF16),
            pltpu.VMEM((2, 4, MSG, T), BF16),
            pltpu.VMEM((2, 3, MSG, T), BF16),
            pltpu.SMEM((2,), jnp.int32),
            pltpu.SemaphoreType.DMA((2 * KINDS,)),
            pltpu.SemaphoreType.DMA((2 * KINDS,)),
            pltpu.SemaphoreType.DMA((9,)),
        ],
        compiler_params=pltpu.CompilerParams(
            collective_id=0, has_side_effects=True, vmem_limit_bytes=56 * 1024 * 1024
        ),
    )(bound, left_query, left_value, right_key, right_value)
    return both[:2], both[2:]


def solution(mesh):
    placed = P("rows", "cols", None)
    return jax.shard_map(
        body,
        mesh=mesh,
        in_specs=(placed, placed, placed, placed, P("rows")),
        out_specs=(placed, placed),
        check_vma=False,
    )
```

```python
import jax
import jax.numpy as jnp
from jax import lax
from jax.experimental import pallas as pl
from jax.experimental.pallas import tpu as pltpu
from jax.sharding import PartitionSpec as P

MESH = pl.DeviceIdType.MESH
F32 = jnp.float32
BF16 = jnp.bfloat16

NX, NY = 4, 8
T, D = 128, 256
STAT = 16
MSG = D + STAT
NEVER = -(2.0**100)
FAR = 1 << 28
SCALE = 1.4426950408889634 / 16.0

AP, B1P, B1M, B2P, B2M, AX = 0, 1, 2, 3, 4, 5
VALUES = 11
PAX, PAP, PBF, PBP, PBM = 22, 28, 29, 30, 31
KINDS = 32


def kernel(
    bound, lq, lv, rk, rv, out,
    ak, av, bk, bv, raw, pa_w, pb_w, sa, sb, oa, ob, stat_a, stat_b,
    pa, ra, passed, rap, pb, rb, bound_ref, send, recv, local,
):
    row = lax.axis_index("rows")
    col = lax.axis_index("cols")
    x, y = col // NY, col % NY

    def at(nx, ny):
        return (row, nx * NY + ny)

    def step_y(d):
        return lax.rem(y + d + NY, NY)

    odd = lax.rem(y, 2)
    partner = [step_y(1 - 2 * odd), step_y(2 * odd - 1)]
    up, down = at(x, step_y(2)), at(x, step_y(-2))
    mate = [at(x, partner[0]), at(x, partner[1])]
    across = [at(lax.rem(x + d, NX), y) for d in (1, 2, 3)]

    keys_a, keys_b = (lq.at[0], rk.at[1]), (rk.at[0], lq.at[1])
    vals_a, vals_b = (lv.at[0], rv.at[1]), (rv.at[0], lv.at[1])
    out_a, out_b = (out.at[0], out.at[3]), (out.at[2], out.at[1])
    lines = [NX - x, x + 1]

    barrier = pltpu.get_barrier_semaphore()
    for device in [up, down] + mate + across:
        pl.semaphore_signal(barrier, inc=1, device_id=device, device_id_type=MESH)

    copies = []
    for t in range(2):
        for src, dst in (
            (keys_a[t], ak.at[t, 0, pl.ds(0, T)]),
            (keys_b[t], bk.at[t, pl.ds(0, T)]),
            (vals_a[t], raw.at[t, 0]),
            (vals_b[t], raw.at[t, 1]),
        ):
            copies.append(pltpu.make_async_copy(src, dst, local.at[len(copies)]))
            copies[-1].start()
    copies.append(pltpu.make_async_copy(bound, bound_ref, local.at[8]))
    copies[-1].start()
    pl.semaphore_wait(barrier, 7)

    def message(t, number, src, dst, device):
        n = t * KINDS + number
        return pltpu.make_async_remote_copy(
            src_ref=src, dst_ref=dst, send_sem=send.at[n], recv_sem=recv.at[n],
            device_id=device, device_id_type=MESH,
        )

    def line(t, d):
        return at(x - d, y) if t == 0 else at(x + d, y)

    def line_in(t, d):
        return x - d >= 0 if t == 0 else x + d < NX

    def ap(t, kv):
        if kv == 0:
            return message(t, AP, keys_a[t], ak.at[t, 0, pl.ds(T, T)], mate[t])
        return message(t, VALUES + AP, av.at[t, 0, 0], av.at[t, 0, 1], mate[t])

    def b_slot(t, kv, s):
        return bk.at[t, pl.ds(s * T, T)] if kv == 0 else bv.at[t, s]

    def b_own(t, kv):
        return keys_b[t] if kv == 0 else bv.at[t, 0]

    def b1p(t, kv):
        return message(t, VALUES * kv + B1P, b_own(t, kv), b_slot(t, kv, 1), up)

    def b1m(t, kv):
        return message(t, VALUES * kv + B1M, b_own(t, kv), b_slot(t, kv, 2), down)

    def b_half(t, kv, s, half):
        if kv == 0:
            return bk.at[t, pl.ds(s * T + half * (T // 2), T // 2)]
        return bv.at[t, s, pl.ds(half * (D // 2), D // 2)]

    def b2p(t, kv):
        return message(t, VALUES * kv + B2P, b_half(t, kv, 1, 0), b_half(t, kv, 3, 0), up)

    def b2m(t, kv):
        return message(t, VALUES * kv + B2M, b_half(t, kv, 2, 1), b_half(t, kv, 3, 1), down)

    def a_half(t, kv, d, h):
        return ak.at[t, d, pl.ds(h * T, T)] if kv == 0 else av.at[t, d, h]

    def ax(t, kv, d, h):
        src = keys_a[t] if kv == 0 and h == 0 else a_half(t, kv, 0, h)
        return message(t, VALUES * kv + AX + 3 * h + d - 1, src, a_half(t, kv, d, h), line(t, d))

    def arrive_a(t, kv, d):
        for h in range(2):
            arrival(
                t, VALUES * kv + AX + 3 * h + d - 1, a_half(t, kv, 0, h), a_half(t, kv, d, h)
            ).wait_recv()

    def pax(t, d, h):
        return message(t, PAX + 3 * h + d - 1, pa.at[t, d, h], ra.at[t, d, h], line(t, -d))

    def pap(t):
        return message(t, PAP, passed.at[t], rap.at[t], mate[t])

    def arrival(t, number, src, dst):
        return message(t, number, src, dst, up)

    def pbf(t):
        return message(t, PBF, pb.at[t, 3], rb.at[t, 0], up if t == 0 else down)

    def pbp(t):
        return message(t, PBP, pb.at[t, 2], rb.at[t, 1], up)

    def pbm(t):
        return message(t, PBM, pb.at[t, 1], rb.at[t, 2], down)

    def each_line(t, act, kv, h):
        for d in (1, 2, 3):
            pl.when(line_in(t, d))(lambda d=d: act(ax(t, kv, d, h)))

    def start(m):
        m.start()

    def load():
        for copy in copies:
            copy.wait()
        for t in range(2):
            av[t, 0, 0] = raw[t, 0].astype(F32).T.astype(BF16)
            bv[t, 0] = raw[t, 1].astype(F32).T.astype(BF16)

    def send_a(t, kv):
        ap(t, kv).start()

    def send_b(t, kv):
        b1p(t, kv).start()
        b1m(t, kv).start()

    def relay_a(t, kv):
        ap(t, kv).wait_recv()
        each_line(t, start, kv, 1)

    def send_x(t, kv):
        each_line(t, start, kv, 0)

    def relay_b(t, kv):
        b1p(t, kv).wait_recv()
        b2p(t, kv).start()
        b1m(t, kv).wait_recv()
        b2m(t, kv).start()

    def rest_b(t, kv):
        b2p(t, kv).wait_recv()
        b2m(t, kv).wait_recv()

    y_b = [y, step_y(-2), step_y(2), step_y(4)]
    diff = lax.broadcasted_iota(jnp.int32, (T, T), 1) - lax.broadcasted_iota(jnp.int32, (T, T), 0)

    def threshold(t, d, s, h):
        y_a = partner[t] if h else y
        ahead = 8 * d + (y_a - y_b[s] if t == 0 else y_b[s] - y_a)
        return jnp.where(ahead <= bound_ref[t], -T * ahead, FAR)

    def scores(t):
        @pl.loop(0, lines[t])
        def _(d):
            @pl.when(d > 0)
            def _():
                arrive_a(t, 0, d)

            a = ak[t, d]
            top = jnp.full((1, 2 * T), NEVER, F32)
            for s in range(4):
                dots = lax.dot_general(
                    bk[t, pl.ds(s * T, T)], a, (((1,), (1,)), ((), ())), preferred_element_type=F32
                ) * SCALE
                for h in range(2):
                    gap = diff if t == 0 else -diff
                    piece = jnp.where(
                        gap >= threshold(t, d, s, h), dots[:, h * T : (h + 1) * T], NEVER
                    )
                    sa[pl.ds(s * T, T), pl.ds(h * T, T)] = piece
            for s in range(4):
                top = jnp.maximum(top, jnp.max(sa[pl.ds(s * T, T)], axis=0, keepdims=True))
            top = top.astype(BF16).astype(F32)
            total = jnp.zeros((1, 2 * T), F32)
            for s in range(4):
                w = jnp.exp2(sa[pl.ds(s * T, T)] - top)
                total = total + jnp.sum(w, axis=0, keepdims=True)
                pa_w[t, d, pl.ds(s * T, T)] = w.astype(BF16)
            stat_a[t, d, 0:1] = top
            stat_a[t, d, 1:2] = total
            for s in range(4):
                dots = lax.dot_general(
                    a, bk[t, pl.ds(s * T, T)], (((1,), (1,)), ((), ())), preferred_element_type=F32
                ) * SCALE
                for h in range(2):
                    gap = -diff if t == 0 else diff
                    sb[d, pl.ds(h * T, T), pl.ds(s * T, T)] = jnp.where(
                        gap >= threshold(t, d, s, h), dots[h * T : (h + 1) * T], NEVER
                    )

        top = lax.fori_loop(
            0, lines[t],
            lambda d, m: jnp.maximum(m, jnp.max(sb[d], axis=0, keepdims=True)),
            jnp.full((1, 4 * T), NEVER, F32),
        )
        top = top.astype(BF16).astype(F32)

        def weigh(d, total):
            w = jnp.exp2(sb[d] - top)
            pb_w[t, d] = w.astype(BF16)
            return total + jnp.sum(w, axis=0, keepdims=True)

        total = lax.fori_loop(0, lines[t], weigh, jnp.zeros((1, 4 * T), F32))
        stat_b[t, 0:1] = top
        stat_b[t, 1:2] = total

    def put(ref, top, total, rows):
        place = lax.broadcasted_iota(jnp.int32, (STAT, rows.shape[1]), 0)
        ref[pl.ds(0, D)] = rows.astype(BF16)
        high = total.astype(BF16).astype(F32)
        stats = jnp.where(place == 0, top, jnp.where(place == 1, high, jnp.where(place == 2, total - high, 0.0)))
        ref[pl.ds(D, STAT)] = stats.astype(BF16)

    def get(ref):
        stats = ref[pl.ds(D, STAT)].astype(F32)
        return stats[0:1], stats[1:2] + stats[2:3], ref[pl.ds(0, D)].astype(F32)

    def b_part(t, s):
        c = pl.ds(s * T, T)
        return stat_b[t, 0:1, c], stat_b[t, 1:2, c], ob[t, :, c]

    def merge(one, two):
        top = jnp.maximum(one[0], two[0])
        a, b = jnp.exp2(one[0] - top), jnp.exp2(two[0] - top)
        return top, one[1] * a + two[1] * b, one[2] * a + two[2] * b

    def sums_b(t):
        ob[t] = jnp.zeros_like(ob[t])

        @pl.loop(0, lines[t])
        def _(d, t=t):
            @pl.when(d > 0)
            def _():
                arrive_a(t, 1, d)

            values = jnp.concatenate([av[t, d, 0], av[t, d, 1]], axis=1)
            ob[t] += jnp.dot(values, pb_w[t, d], preferred_element_type=F32)

        put(pb.at[t, 3], *b_part(t, 3))
        pbf(t).start()

    def direct_b(t):
        put(pb.at[t, 1 + t], *b_part(t, 1 + t))
        (pbm if t == 0 else pbp)(t).start()

    def sums_a(t):
        @pl.loop(0, lines[t])
        def _(d, t=t):
            values = jnp.concatenate([bv[t, s] for s in range(4)], axis=1)
            rows = jnp.dot(values, pa_w[t, d], preferred_element_type=F32)

            @pl.when(d == 0)
            def _():
                oa[t] = rows

            @pl.when(d > 0)
            def _():
                for h in range(2):
                    c = slice(h * T, (h + 1) * T)
                    put(pa.at[t, d, h], stat_a[t, d, 0:1, c], stat_a[t, d, 1:2, c], rows[:, c])
                pax(t, d, 1).start()

    def own_a(t):
        @pl.loop(1, lines[t])
        def _(d):
            pax(t, d, 0).start()

    def pass_b(t):
        pbf(t).wait_recv()
        put(pb.at[t, 2 - t], *merge(b_part(t, 2 - t), get(rb.at[t, 0])))
        (pbp if t == 0 else pbm)(t).start()

    def add_a(t, h):
        c = slice(h * T, (h + 1) * T)

        @pl.loop(1, NX + 1 - lines[t])
        def _(d):
            arrival(t, PAX + 3 * h + d - 1, pa.at[t, d, h], ra.at[t, d, h]).wait_recv()
            own = stat_a[t, 0, 0:1, c], stat_a[t, 0, 1:2, c], oa[t, :, c]
            top, total, rows = merge(own, get(ra.at[t, d, h]))
            stat_a[t, 0, 0:1, c] = top
            stat_a[t, 0, 1:2, c] = total
            oa[t, :, c] = rows

    def pass_a(t):
        add_a(t, 1)
        put(passed.at[t], stat_a[t, 0, 0:1, T:], stat_a[t, 0, 1:2, T:], oa[t, :, T:])
        pap(t).start()

    def finish(ref, part):
        ref[...] = (part[2] * (1.0 / part[1])).T.astype(BF16)

    def last_b(t):
        pbp(t).wait_recv()
        pbm(t).wait_recv()
        finish(out_b[t], merge(merge(b_part(t, 0), get(rb.at[t, 1])), get(rb.at[t, 2])))
    def last_a(t):
        add_a(t, 0)
        pap(t).wait_recv()
        own = stat_a[t, 0, 0:1, :T], stat_a[t, 0, 1:2, :T], oa[t, :, :T]
        finish(out_a[t], merge(own, get(rap.at[t])))

    def left_b(t, kv):
        b1p(t, kv).wait_send()
        b1m(t, kv).wait_send()

    send_b(0, 0)
    send_b(1, 0)
    send_a(0, 0)
    send_a(1, 0)
    send_x(0, 0)
    send_x(1, 0)
    load()
    send_a(0, 1)
    send_a(1, 1)
    send_x(0, 1)
    send_x(1, 1)
    send_b(0, 1)
    send_b(1, 1)
    relay_a(0, 0)
    relay_a(1, 0)
    relay_a(0, 1)
    relay_a(1, 1)
    relay_b(0, 0)
    relay_b(1, 0)
    relay_b(0, 1)
    relay_b(1, 1)
    rest_b(0, 0)
    scores(0)
    sums_b(0)
    rest_b(1, 0)
    scores(1)
    sums_b(1)
    rest_b(0, 1)
    rest_b(1, 1)
    sums_a(0)
    sums_a(1)
    own_a(0)
    own_a(1)
    direct_b(0)
    direct_b(1)
    pass_b(0)
    pass_b(1)
    pass_a(0)
    pass_a(1)
    last_b(0)
    last_b(1)
    last_a(0)
    last_a(1)

    for t in range(2):
        for kv in range(2):
            for m in (ap, b1p, b1m, b2p, b2m):
                m(t, kv).wait_send()
            for h in range(2):
                each_line(t, lambda m: m.wait_send(), kv, h)
        for m in (pbf, pbp, pbm, pap):
            m(t).wait_send()

        @pl.loop(1, lines[t])
        def _(d, t=t):
            pax(t, d, 0).wait_send()
            pax(t, d, 1).wait_send()


def body(left_query, left_value, right_key, right_value, bound):
    hbm = pl.BlockSpec(memory_space=pl.ANY)
    vmem = pl.BlockSpec(memory_space=pltpu.VMEM)
    both = pl.pallas_call(
        kernel,
        out_shape=jax.ShapeDtypeStruct((4, T, D), BF16),
        in_specs=[hbm] * 5,
        out_specs=vmem,
        scratch_shapes=[
            pltpu.VMEM((2, NX, 2 * T, D), BF16),
            pltpu.VMEM((2, NX, 2, D, T), BF16),
            pltpu.VMEM((2, 4 * T, D), BF16),
            pltpu.VMEM((2, 4, D, T), BF16),
            pltpu.VMEM((2, 2, T, D), BF16),
            pltpu.VMEM((2, NX, 4 * T, 2 * T), BF16),
            pltpu.VMEM((2, NX, 2 * T, 4 * T), BF16),
            pltpu.VMEM((4 * T, 2 * T), F32),
            pltpu.VMEM((NX, 2 * T, 4 * T), F32),
            pltpu.VMEM((2, D, 2 * T), F32),
            pltpu.VMEM((2, D, 4 * T), F32),
            pltpu.VMEM((2, NX, 8, 2 * T), F32),
            pltpu.VMEM((2, 8, 4 * T), F32),
            pltpu.VMEM((2, NX, 2, MSG, T), BF16),
            pltpu.VMEM((2, NX, 2, MSG, T), BF16),
            pltpu.VMEM((2, MSG, T), BF16),
            pltpu.VMEM((2, MSG, T), BF16),
            pltpu.VMEM((2, 4, MSG, T), BF16),
            pltpu.VMEM((2, 3, MSG, T), BF16),
            pltpu.SMEM((2,), jnp.int32),
            pltpu.SemaphoreType.DMA((2 * KINDS,)),
            pltpu.SemaphoreType.DMA((2 * KINDS,)),
            pltpu.SemaphoreType.DMA((9,)),
        ],
        compiler_params=pltpu.CompilerParams(
            collective_id=0, has_side_effects=True, vmem_limit_bytes=56 * 1024 * 1024
        ),
    )(bound, left_query, left_value, right_key, right_value)
    return both[:2], both[2:]


def solution(mesh):
    placed = P("rows", "cols", None)
    return jax.shard_map(
        body,
        mesh=mesh,
        in_specs=(placed, placed, placed, placed, P("rows")),
        out_specs=(placed, placed),
        check_vma=False,
    )
```

```python
import jax
import jax.numpy as jnp
from jax import lax
from jax.experimental import pallas as pl
from jax.experimental.pallas import tpu as pltpu
from jax.sharding import PartitionSpec as P

MESH = pl.DeviceIdType.MESH
F32 = jnp.float32
BF16 = jnp.bfloat16

NX, NY = 4, 8
T, D = 128, 256
STAT = 16
MSG = D + STAT
NEVER = -(2.0**100)
FAR = 1 << 28
SCALE = 1.4426950408889634 / 16.0

AP, B1P, B1M, B2P, B2M, AX = 0, 1, 2, 3, 4, 5
VALUES = 11
PAX, PAP, PBF, PBP, PBM = 22, 28, 29, 30, 31
KINDS = 32


def kernel(
    bound, lq, lv, rk, rv, out,
    ak, av, bk, bv, raw, pa_w, pb_w, sa, sb, oa, ob, stat_a, stat_b,
    pa, ra, passed, rap, pb, rb, bound_ref, send, recv, local,
):
    row = lax.axis_index("rows")
    col = lax.axis_index("cols")
    x, y = col // NY, col % NY

    def at(nx, ny):
        return (row, nx * NY + ny)

    def step_y(d):
        return lax.rem(y + d + NY, NY)

    odd = lax.rem(y, 2)
    partner = [step_y(1 - 2 * odd), step_y(2 * odd - 1)]
    up, down = at(x, step_y(2)), at(x, step_y(-2))
    mate = [at(x, partner[0]), at(x, partner[1])]
    across = [at(lax.rem(x + d, NX), y) for d in (1, 2, 3)]

    keys_a, keys_b = (lq.at[0], rk.at[1]), (rk.at[0], lq.at[1])
    vals_a, vals_b = (lv.at[0], rv.at[1]), (rv.at[0], lv.at[1])
    out_a, out_b = (out.at[0], out.at[3]), (out.at[2], out.at[1])
    lines = [NX - x, x + 1]

    barrier = pltpu.get_barrier_semaphore()
    for device in [up, down] + mate + across:
        pl.semaphore_signal(barrier, inc=1, device_id=device, device_id_type=MESH)

    copies = []
    for t in range(2):
        for src, dst in (
            (keys_a[t], ak.at[t, 0, pl.ds(0, T)]),
            (keys_b[t], bk.at[t, pl.ds(0, T)]),
            (vals_a[t], raw.at[t, 0]),
            (vals_b[t], raw.at[t, 1]),
        ):
            copies.append(pltpu.make_async_copy(src, dst, local.at[len(copies)]))
            copies[-1].start()
    copies.append(pltpu.make_async_copy(bound, bound_ref, local.at[8]))
    copies[-1].start()
    pl.semaphore_wait(barrier, 7)

    def message(t, number, src, dst, device):
        n = t * KINDS + number
        return pltpu.make_async_remote_copy(
            src_ref=src, dst_ref=dst, send_sem=send.at[n], recv_sem=recv.at[n],
            device_id=device, device_id_type=MESH,
        )

    def line(t, d):
        return at(x - d, y) if t == 0 else at(x + d, y)

    def line_in(t, d):
        return x - d >= 0 if t == 0 else x + d < NX

    def ap(t, kv):
        if kv == 0:
            return message(t, AP, keys_a[t], ak.at[t, 0, pl.ds(T, T)], mate[t])
        return message(t, VALUES + AP, av.at[t, 0, 0], av.at[t, 0, 1], mate[t])

    def b_slot(t, kv, s):
        return bk.at[t, pl.ds(s * T, T)] if kv == 0 else bv.at[t, s]

    def b_own(t, kv):
        return keys_b[t] if kv == 0 else bv.at[t, 0]

    def b1p(t, kv):
        return message(t, VALUES * kv + B1P, b_own(t, kv), b_slot(t, kv, 1), up)

    def b1m(t, kv):
        return message(t, VALUES * kv + B1M, b_own(t, kv), b_slot(t, kv, 2), down)

    def b_half(t, kv, s, half):
        if kv == 0:
            return bk.at[t, pl.ds(s * T + half * (T // 2), T // 2)]
        return bv.at[t, s, pl.ds(half * (D // 2), D // 2)]

    def b2p(t, kv):
        return message(t, VALUES * kv + B2P, b_half(t, kv, 1, 0), b_half(t, kv, 3, 0), up)

    def b2m(t, kv):
        return message(t, VALUES * kv + B2M, b_half(t, kv, 2, 1), b_half(t, kv, 3, 1), down)

    def a_half(t, kv, d, h):
        return ak.at[t, d, pl.ds(h * T, T)] if kv == 0 else av.at[t, d, h]

    def ax(t, kv, d, h):
        src = keys_a[t] if kv == 0 and h == 0 else a_half(t, kv, 0, h)
        return message(t, VALUES * kv + AX + 3 * h + d - 1, src, a_half(t, kv, d, h), line(t, d))

    def arrive_a(t, kv, d):
        for h in range(2):
            arrival(
                t, VALUES * kv + AX + 3 * h + d - 1, a_half(t, kv, 0, h), a_half(t, kv, d, h)
            ).wait_recv()

    def pax(t, d, h):
        return message(t, PAX + 3 * h + d - 1, pa.at[t, d, h], ra.at[t, d, h], line(t, -d))

    def pap(t):
        return message(t, PAP, passed.at[t], rap.at[t], mate[t])

    def arrival(t, number, src, dst):
        return message(t, number, src, dst, up)

    def pbf(t):
        return message(t, PBF, pb.at[t, 3], rb.at[t, 0], up if t == 0 else down)

    def pbp(t):
        return message(t, PBP, pb.at[t, 2], rb.at[t, 1], up)

    def pbm(t):
        return message(t, PBM, pb.at[t, 1], rb.at[t, 2], down)

    def each_line(t, act, kv, h):
        for d in (1, 2, 3):
            pl.when(line_in(t, d))(lambda d=d: act(ax(t, kv, d, h)))

    def start(m):
        m.start()

    def load():
        for copy in copies:
            copy.wait()
        for t in range(2):
            av[t, 0, 0] = raw[t, 0].astype(F32).T.astype(BF16)
            bv[t, 0] = raw[t, 1].astype(F32).T.astype(BF16)

    def send_a(t, kv):
        ap(t, kv).start()

    def send_b(t, kv):
        b1p(t, kv).start()
        b1m(t, kv).start()

    def relay_a(t, kv):
        ap(t, kv).wait_recv()
        each_line(t, start, kv, 1)

    def send_x(t, kv):
        each_line(t, start, kv, 0)

    def relay_b(t, kv):
        b1p(t, kv).wait_recv()
        b2p(t, kv).start()
        b1m(t, kv).wait_recv()
        b2m(t, kv).start()

    def rest_b(t, kv):
        b2p(t, kv).wait_recv()
        b2m(t, kv).wait_recv()

    y_b = [y, step_y(-2), step_y(2), step_y(4)]
    diff = lax.broadcasted_iota(jnp.int32, (T, T), 1) - lax.broadcasted_iota(jnp.int32, (T, T), 0)

    def threshold(t, d, s, h):
        y_a = partner[t] if h else y
        ahead = 8 * d + (y_a - y_b[s] if t == 0 else y_b[s] - y_a)
        return jnp.where(ahead <= bound_ref[t], -T * ahead, FAR)

    def scores(t):
        @pl.loop(0, lines[t])
        def _(d):
            @pl.when(d > 0)
            def _():
                arrive_a(t, 0, d)

            a = ak[t, d]
            for s in range(4):
                dots = lax.dot_general(
                    a, bk[t, pl.ds(s * T, T)], (((1,), (1,)), ((), ())), preferred_element_type=F32
                ) * SCALE
                for h in range(2):
                    gap = -diff if t == 0 else diff
                    sb[d, pl.ds(h * T, T), pl.ds(s * T, T)] = jnp.where(
                        gap >= threshold(t, d, s, h), dots[h * T : (h + 1) * T], NEVER
                    )

        top = lax.fori_loop(
            0, lines[t],
            lambda d, m: jnp.maximum(m, jnp.max(sb[d], axis=0, keepdims=True)),
            jnp.full((1, 4 * T), NEVER, F32),
        )
        top = top.astype(BF16).astype(F32)

        def weigh(d, total):
            w = jnp.exp2(sb[d] - top)
            pb_w[t, d] = w.astype(BF16)
            return total + jnp.sum(w, axis=0, keepdims=True)

        total = lax.fori_loop(0, lines[t], weigh, jnp.zeros((1, 4 * T), F32))
        stat_b[t, 0:1] = top
        stat_b[t, 1:2] = total

    def scores_a(t):
        @pl.loop(0, lines[t])
        def _(d):
            a = ak[t, d]
            top = jnp.full((1, 2 * T), NEVER, F32)
            for s in range(4):
                dots = lax.dot_general(
                    bk[t, pl.ds(s * T, T)], a, (((1,), (1,)), ((), ())), preferred_element_type=F32
                ) * SCALE
                for h in range(2):
                    gap = diff if t == 0 else -diff
                    piece = jnp.where(
                        gap >= threshold(t, d, s, h), dots[:, h * T : (h + 1) * T], NEVER
                    )
                    sa[pl.ds(s * T, T), pl.ds(h * T, T)] = piece
            for s in range(4):
                top = jnp.maximum(top, jnp.max(sa[pl.ds(s * T, T)], axis=0, keepdims=True))
            top = top.astype(BF16).astype(F32)
            total = jnp.zeros((1, 2 * T), F32)
            for s in range(4):
                w = jnp.exp2(sa[pl.ds(s * T, T)] - top)
                total = total + jnp.sum(w, axis=0, keepdims=True)
                pa_w[t, d, pl.ds(s * T, T)] = w.astype(BF16)
            stat_a[t, d, 0:1] = top
            stat_a[t, d, 1:2] = total

    def put(ref, top, total, rows):
        place = lax.broadcasted_iota(jnp.int32, (STAT, rows.shape[1]), 0)
        ref[pl.ds(0, D)] = rows.astype(BF16)
        high = total.astype(BF16).astype(F32)
        stats = jnp.where(place == 0, top, jnp.where(place == 1, high, jnp.where(place == 2, total - high, 0.0)))
        ref[pl.ds(D, STAT)] = stats.astype(BF16)

    def get(ref):
        stats = ref[pl.ds(D, STAT)].astype(F32)
        return stats[0:1], stats[1:2] + stats[2:3], ref[pl.ds(0, D)].astype(F32)

    def b_part(t, s):
        c = pl.ds(s * T, T)
        return stat_b[t, 0:1, c], stat_b[t, 1:2, c], ob[t, :, c]

    def merge(one, two):
        top = jnp.maximum(one[0], two[0])
        a, b = jnp.exp2(one[0] - top), jnp.exp2(two[0] - top)
        return top, one[1] * a + two[1] * b, one[2] * a + two[2] * b

    def sums_b(t):
        ob[t] = jnp.zeros_like(ob[t])

        @pl.loop(0, lines[t])
        def _(d, t=t):
            @pl.when(d > 0)
            def _():
                arrive_a(t, 1, d)

            values = jnp.concatenate([av[t, d, 0], av[t, d, 1]], axis=1)
            ob[t] += jnp.dot(values, pb_w[t, d], preferred_element_type=F32)

        put(pb.at[t, 3], *b_part(t, 3))
        pbf(t).start()

    def direct_b(t):
        put(pb.at[t, 1 + t], *b_part(t, 1 + t))
        (pbm if t == 0 else pbp)(t).start()

    def sums_a(t):
        @pl.loop(0, lines[t])
        def _(d, t=t):
            values = jnp.concatenate([bv[t, s] for s in range(4)], axis=1)
            rows = jnp.dot(values, pa_w[t, d], preferred_element_type=F32)

            @pl.when(d == 0)
            def _():
                oa[t] = rows

            @pl.when(d > 0)
            def _():
                for h in range(2):
                    c = slice(h * T, (h + 1) * T)
                    put(pa.at[t, d, h], stat_a[t, d, 0:1, c], stat_a[t, d, 1:2, c], rows[:, c])
                pax(t, d, 1).start()

    def own_a(t):
        @pl.loop(1, lines[t])
        def _(d):
            pax(t, d, 0).start()

    def pass_b(t):
        pbf(t).wait_recv()
        put(pb.at[t, 2 - t], *merge(b_part(t, 2 - t), get(rb.at[t, 0])))
        (pbp if t == 0 else pbm)(t).start()

    def add_a(t, h):
        c = slice(h * T, (h + 1) * T)

        @pl.loop(1, NX + 1 - lines[t])
        def _(d):
            arrival(t, PAX + 3 * h + d - 1, pa.at[t, d, h], ra.at[t, d, h]).wait_recv()
            own = stat_a[t, 0, 0:1, c], stat_a[t, 0, 1:2, c], oa[t, :, c]
            top, total, rows = merge(own, get(ra.at[t, d, h]))
            stat_a[t, 0, 0:1, c] = top
            stat_a[t, 0, 1:2, c] = total
            oa[t, :, c] = rows

    def pass_a(t):
        add_a(t, 1)
        put(passed.at[t], stat_a[t, 0, 0:1, T:], stat_a[t, 0, 1:2, T:], oa[t, :, T:])
        pap(t).start()

    def finish(ref, part):
        ref[...] = (part[2] * (1.0 / part[1])).T.astype(BF16)

    def last_b(t):
        pbp(t).wait_recv()
        pbm(t).wait_recv()
        finish(out_b[t], merge(merge(b_part(t, 0), get(rb.at[t, 1])), get(rb.at[t, 2])))
    def last_a(t):
        add_a(t, 0)
        pap(t).wait_recv()
        own = stat_a[t, 0, 0:1, :T], stat_a[t, 0, 1:2, :T], oa[t, :, :T]
        finish(out_a[t], merge(own, get(rap.at[t])))

    def left_b(t, kv):
        b1p(t, kv).wait_send()
        b1m(t, kv).wait_send()

    send_b(0, 0)
    send_b(1, 0)
    send_a(0, 0)
    send_a(1, 0)
    send_x(0, 0)
    send_x(1, 0)
    load()
    send_a(0, 1)
    send_a(1, 1)
    send_x(0, 1)
    send_x(1, 1)
    send_b(0, 1)
    send_b(1, 1)
    relay_a(0, 0)
    relay_a(1, 0)
    relay_a(0, 1)
    relay_a(1, 1)
    relay_b(0, 0)
    relay_b(1, 0)
    relay_b(0, 1)
    relay_b(1, 1)
    rest_b(0, 0)
    scores(0)
    sums_b(0)
    rest_b(1, 0)
    scores(1)
    sums_b(1)
    scores_a(0)
    scores_a(1)
    rest_b(0, 1)
    rest_b(1, 1)
    sums_a(0)
    sums_a(1)
    own_a(0)
    own_a(1)
    direct_b(0)
    direct_b(1)
    pass_b(0)
    pass_b(1)
    pass_a(0)
    pass_a(1)
    last_b(0)
    last_b(1)
    last_a(0)
    last_a(1)

    for t in range(2):
        for kv in range(2):
            for m in (ap, b1p, b1m, b2p, b2m):
                m(t, kv).wait_send()
            for h in range(2):
                each_line(t, lambda m: m.wait_send(), kv, h)
        for m in (pbf, pbp, pbm, pap):
            m(t).wait_send()

        @pl.loop(1, lines[t])
        def _(d, t=t):
            pax(t, d, 0).wait_send()
            pax(t, d, 1).wait_send()


def body(left_query, left_value, right_key, right_value, bound):
    hbm = pl.BlockSpec(memory_space=pl.ANY)
    vmem = pl.BlockSpec(memory_space=pltpu.VMEM)
    both = pl.pallas_call(
        kernel,
        out_shape=jax.ShapeDtypeStruct((4, T, D), BF16),
        in_specs=[hbm] * 5,
        out_specs=vmem,
        scratch_shapes=[
            pltpu.VMEM((2, NX, 2 * T, D), BF16),
            pltpu.VMEM((2, NX, 2, D, T), BF16),
            pltpu.VMEM((2, 4 * T, D), BF16),
            pltpu.VMEM((2, 4, D, T), BF16),
            pltpu.VMEM((2, 2, T, D), BF16),
            pltpu.VMEM((2, NX, 4 * T, 2 * T), BF16),
            pltpu.VMEM((2, NX, 2 * T, 4 * T), BF16),
            pltpu.VMEM((4 * T, 2 * T), F32),
            pltpu.VMEM((NX, 2 * T, 4 * T), F32),
            pltpu.VMEM((2, D, 2 * T), F32),
            pltpu.VMEM((2, D, 4 * T), F32),
            pltpu.VMEM((2, NX, 8, 2 * T), F32),
            pltpu.VMEM((2, 8, 4 * T), F32),
            pltpu.VMEM((2, NX, 2, MSG, T), BF16),
            pltpu.VMEM((2, NX, 2, MSG, T), BF16),
            pltpu.VMEM((2, MSG, T), BF16),
            pltpu.VMEM((2, MSG, T), BF16),
            pltpu.VMEM((2, 4, MSG, T), BF16),
            pltpu.VMEM((2, 3, MSG, T), BF16),
            pltpu.SMEM((2,), jnp.int32),
            pltpu.SemaphoreType.DMA((2 * KINDS,)),
            pltpu.SemaphoreType.DMA((2 * KINDS,)),
            pltpu.SemaphoreType.DMA((9,)),
        ],
        compiler_params=pltpu.CompilerParams(
            collective_id=0, has_side_effects=True, vmem_limit_bytes=56 * 1024 * 1024
        ),
    )(bound, left_query, left_value, right_key, right_value)
    return both[:2], both[2:]


def solution(mesh):
    placed = P("rows", "cols", None)
    return jax.shard_map(
        body,
        mesh=mesh,
        in_specs=(placed, placed, placed, placed, P("rows")),
        out_specs=(placed, placed),
        check_vma=False,
    )
```
